32 devices in a mesh: seq: 8 (over y, x, core), head: 4 (over z).
Axes of the slice: x: 2, y: 2, z: 4, core: 2. Of those that a mesh axis runs over, the one named last changes fastest.
Arguments:
- queries: bfloat16 [2048, 12288], P('seq', 'head'), may hold values from -256 to 256
- own_latent: bfloat16 [2048, 576], P('seq'), may hold values from -16 to 16
- cache: bfloat16 [256, 128, 576], P('seq', 'head'), may hold values from -6 to 6
- block_list: int32 [8, 32], replicated, may hold values from 0 to 255, as said below
- offsets: int32 [8, 32], P('seq'), may hold values from -4096 to 4096
- tile_mask: int32 [8, 2, 32], P('seq'), may hold values 0 or 1
- w_uk: bfloat16 [64, 128, 512], P('head'), may hold values from -0.5 to 0.5
- w_uv: bfloat16 [64, 512, 128], P('head'), may hold values from -0.25 to 0.25
- w_o: bfloat16 [8192, 7168], P('head'), may hold values from -0.0625 to 0.0625
Outputs:
- layer_out: bfloat16 [2048, 7168], P('seq', 'head')
The draws below stay inside these ranges and needn't reach their ends.
Inputs may be any that keep to these rules, and one draw needn't show every extreme that they name: `block_list`: entry (r, j) names a pooled span whose owner is index entry // 32 of seq. In each row no owner is named more than 4 times, and at least one owner is named exactly 4 times.
All inputs are finite; a program needn't handle non-finite values. No bound on the sum of `tile_mask` on one device may be relied on, other than what follows from the above.
Results may differ from the reference program's by a relative error of at most 0.015.
Values may be sent and summed in bfloat16 or wider, within the bound.
A program may use at most 128 MiB of HBM per device.

```python
import jax
import jax.numpy as jnp
from jax import lax

D = 7168
HEADS = 64
NOPE = 128
ROPE = 64
V = 128
LAT = 512
SLAB = 256
SPAN_DEV = 32
SPAN = 128
LISTED = 32
MOST = 4
TOKENS = 2048
QTILES = 2
N_SEQ = 8
N_HEAD = 4


def drawn_pair(key):
    base = jax.random.fold_in(key, 4049)
    keys_list = jax.random.split(base, 3)
    latent = jnp.clip(jax.random.normal(keys_list[0], (TOKENS, LAT + ROPE), jnp.float32), -6.0, 6.0)
    nope_part = jnp.clip(jax.random.normal(keys_list[1], (TOKENS, HEADS, NOPE), jnp.float32), -6.0, 6.0)
    rope_query = jnp.clip(jax.random.normal(keys_list[2], (TOKENS, HEADS, ROPE), jnp.float32), -6.0, 6.0)
    query = jnp.concatenate([nope_part, rope_query], axis=2).reshape(TOKENS, HEADS * (NOPE + ROPE))
    return (jnp.clip(latent, -16.0, 16.0), jnp.clip(query, -256.0, 256.0))


def draw_queries(key, part):
    return drawn_pair(key)[1].astype(jnp.bfloat16)


def draw_own_latent(key, part):
    return drawn_pair(key)[0].astype(jnp.bfloat16)


def draw_block_list(key, part):
    base = jax.random.fold_in(key, 7)

    def one_row(row_key):
        key_owner, key_slots, key_order, key_span = jax.random.split(row_key, 4)
        leading = jax.random.randint(key_owner, (), 0, N_SEQ)
        slot_order = jax.random.permutation(key_slots, (N_SEQ - 1) * MOST)
        others = slot_order[:LISTED - MOST] // MOST
        others = others + (others >= leading).astype(jnp.int32)
        owners = jnp.concatenate([jnp.full((MOST,), leading, jnp.int32), others.astype(jnp.int32)])
        owners = jax.random.permutation(key_order, owners)
        within = jax.random.randint(key_span, (LISTED,), 0, SPAN_DEV)
        return (owners * SPAN_DEV + within).astype(jnp.int32)
    return jax.vmap(one_row)(jax.random.split(base, N_SEQ))


def plant(values, stream_key, smallest, top_value):
    extent = values.shape
    spot = [jax.random.randint(jax.random.fold_in(stream_key, axis), (), 0, extent[axis]) for axis in range(len(extent))]
    values = values.at[tuple(spot)].set(smallest)
    longest = extent.index(max(extent))
    spot[longest] = (spot[longest] + 1) % extent[longest]
    return values.at[tuple(spot)].set(top_value)


def shard_levels(key, shape, cuts, least, largest):
    factor_of = 1.0
    for dim, blocks in cuts:
        steps = jax.random.uniform(jax.random.fold_in(jax.random.fold_in(key, 6), dim), (blocks,), jnp.float32, least / len(cuts), largest / len(cuts))
        factor_of = factor_of * jnp.repeat(jnp.exp(steps), shape[dim] // blocks).reshape((-1,) + (1,) * (len(shape) - 1 - dim))
    return factor_of


def noise(own_key, shape, spread, most, shards=(), kind=jnp.bfloat16):
    values = spread * jax.random.normal(own_key, shape, jnp.float32)
    if shards:
        values = values * shard_levels(own_key, shape, shards, -0.22, 0.18)
    return jnp.clip(values, -most, most).astype(kind)


def setup_inputs(seed: int = 0) -> dict:
    arg_keys = jax.random.split(jax.random.key(seed), 10)
    return {
        "queries": draw_queries(jax.random.fold_in(arg_keys[9], 71), 0),
        "own_latent": draw_own_latent(jax.random.fold_in(arg_keys[9], 71), 0),
        "cache": noise(arg_keys[2], (SPAN_DEV * N_SEQ, SPAN, LAT + ROPE), 1.0, 6.0, ((0, 8), (1, 4))),
        "block_list": draw_block_list(jax.random.fold_in(arg_keys[9], 71), 0),
        "offsets": plant(jax.random.randint(arg_keys[4], (N_SEQ, LISTED), -4096, 4097), jax.random.fold_in(arg_keys[4], 1), -4096, 4096).astype(jnp.int32),
        "tile_mask": plant((jax.random.randint(arg_keys[5], (N_SEQ, QTILES, LISTED), 0, 5) < 3).astype(jnp.int32), jax.random.fold_in(arg_keys[5], 1), 0, 1),
        "w_uk": noise(arg_keys[6], (HEADS, NOPE, LAT), NOPE ** -0.5, 0.5, ((0, 4),)),
        "w_uv": noise(arg_keys[7], (HEADS, LAT, V), LAT ** -0.5, 0.25, ((0, 4),)),
        "w_o": noise(arg_keys[8], (HEADS * V, D), (HEADS * V) ** -0.5, 0.0625, ((0, 4),)),
    }


THETA = 50000.0


def rerotate(blocks, shift):
    halfway = ROPE // 2
    inverse = THETA ** (-jnp.arange(halfway, dtype=jnp.float32) * 2.0 / ROPE)
    angles = shift.astype(jnp.float32)[:, None] * inverse[None, :]
    cosine_table = jnp.cos(angles)[:, None, :]
    sine_table = jnp.sin(angles)[:, None, :]
    rotary = blocks[..., LAT:].astype(jnp.float32)
    first_half = rotary[..., :halfway]
    second_half = rotary[..., halfway:]
    turned = jnp.concatenate([first_half * cosine_table - second_half * sine_table, second_half * cosine_table + first_half * sine_table], axis=-1)
    return jnp.concatenate([blocks[..., :LAT], turned.astype(jnp.bfloat16)], axis=-1)


def allowed_keys(tiles, query_rows, block_rows):
    listed_mask = jnp.repeat(jnp.repeat(tiles > 0, block_rows, axis=0), block_rows, axis=1)
    causal = jnp.tril(jnp.ones((query_rows, query_rows), jnp.bool_))
    return jnp.concatenate([causal, listed_mask], axis=1)


def attend(grouped, context, allowed, key_maps, value_maps):
    nope_width = key_maps.shape[1]
    latent_width = key_maps.shape[2]
    factor = grouped.shape[-1] ** -0.5
    value_latent = context[:, :latent_width]

    def one_head(inputs):
        head_query, key_map, value_map = inputs
        query_latent = jnp.dot(head_query[:, :nope_width], key_map, preferred_element_type=jnp.float32).astype(jnp.bfloat16)
        query_full = jnp.concatenate([query_latent, head_query[:, nope_width:]], axis=1)
        scores = lax.dot_general(query_full, context, (((1,), (1,)), ((), ())), preferred_element_type=jnp.float32) * factor
        scores = jnp.where(allowed, scores, -1e30)
        highest = jnp.max(scores, axis=1, keepdims=True)
        weights = jnp.exp(scores - highest)
        denominator = jnp.sum(weights, axis=1, keepdims=True)
        shares = (weights / denominator).astype(jnp.bfloat16)
        mixed_latent = jnp.dot(shares, value_latent, preferred_element_type=jnp.float32).astype(jnp.bfloat16)
        return jnp.dot(mixed_latent, value_map, preferred_element_type=jnp.float32).astype(jnp.bfloat16)

    per_head = lax.map(one_head, (jnp.transpose(grouped, (1, 0, 2)), key_maps, value_maps))
    return jnp.transpose(per_head, (1, 0, 2)).reshape(grouped.shape[0], -1)


def reference(queries, own_latent, cache, block_list, offsets, tile_mask, w_uk, w_uv, w_o):
    slab_queries = queries.reshape(N_SEQ, SLAB, HEADS, NOPE + ROPE)
    slab_latent = own_latent.reshape(N_SEQ, SLAB, LAT + ROPE)

    def one_slab(inputs):
        grouped, own_rows, listing, shifts, tiles = inputs
        blocks = rerotate(cache[listing], shifts).reshape(LISTED * SPAN, LAT + ROPE)
        context = jnp.concatenate([own_rows, blocks], axis=0)
        allowed = allowed_keys(tiles, SLAB, SPAN)
        head_out = attend(grouped, context, allowed, w_uk, w_uv)
        split_out = head_out.reshape(SLAB, N_HEAD, -1).astype(jnp.float32)
        split_proj = w_o.reshape(N_HEAD, -1, D).astype(jnp.float32)
        partials = jnp.einsum("sgk,gkd->gsd", split_out, split_proj).astype(jnp.bfloat16)
        partials = lax.optimization_barrier(partials)
        return jnp.sum(partials.astype(jnp.float32), axis=0).astype(jnp.bfloat16)

    result = lax.map(one_slab, (slab_queries, slab_latent, block_list, offsets, tile_mask))
    return result.reshape(N_SEQ * SLAB, D)
```

```python
import functools
import math

import jax
import jax.numpy as jnp
from jax import lax
from jax.experimental import pallas as pl
from jax.experimental.pallas import tpu as pltpu
from jax.sharding import PartitionSpec as P

MOST = 4
THETA = 50000.0
MESH = pl.DeviceIdType.MESH
NEG = -1e30


def rotate(rotary, shift):
    width = rotary.shape[-1]
    halfway = width // 2
    inverse = THETA ** (-jnp.arange(halfway, dtype=jnp.float32) * 2.0 / width)
    angles = shift.astype(jnp.float32)[:, None] * inverse[None, :]
    cosine = jnp.cos(angles)[:, None, :]
    sine = jnp.sin(angles)[:, None, :]
    rotary = rotary.astype(jnp.float32)
    first = rotary[..., :halfway]
    second = rotary[..., halfway:]
    turned = jnp.concatenate(
        [first * cosine - second * sine, second * cosine + first * sine], axis=-1
    )
    return turned.astype(jnp.bfloat16)


def attention_kernel(
    n, group, scale,
    lat_in, rope_in, own_lat, own_rope, bias_in, qlat_in, qrest_in, wuv_in,
    out_ref,
    lat, rope, own_l, own_r, bias, qlat, qrest, wuv, acc, top, total,
    load_sem, recv_lat, recv_rope, send_lat, send_rope,
):
    seq = lax.axis_index("seq")
    me = lax.axis_index("head")
    heads, rows, width = qlat.shape
    keys = lat.shape[2]
    steps = heads // group

    mine = [
        pltpu.make_async_copy(lat_in, lat.at[me], load_sem.at[0]),
        pltpu.make_async_copy(rope_in, rope.at[me], load_sem.at[1]),
    ]
    rest = [
        pltpu.make_async_copy(src, dst, load_sem.at[2 + i])
        for i, (src, dst) in enumerate(
            [(own_lat, own_l), (own_rope, own_r), (bias_in, bias), (qlat_in, qlat),
             (qrest_in, qrest), (wuv_in, wuv)]
        )
    ]
    for copy in mine + rest:
        copy.start()

    barrier = pltpu.get_barrier_semaphore()

    @pl.when(me > 0)
    def _():
        pl.semaphore_signal(barrier, inc=1, device_id=(seq, me - 1), device_id_type=MESH)

    @pl.when(me < n - 1)
    def _():
        pl.semaphore_signal(barrier, inc=1, device_id=(seq, me + 1), device_id_type=MESH)

    peers = jnp.where(me > 0, 1, 0) + jnp.where(me < n - 1, 1, 0)
    pl.semaphore_wait(barrier, peers)

    for copy in mine:
        copy.wait()

    def latent_copy(origin, half, way):
        return pltpu.make_async_remote_copy(
            src_ref=lat.at[origin, half], dst_ref=lat.at[origin, half],
            send_sem=send_lat.at[way, origin, half], recv_sem=recv_lat.at[origin, half],
            device_id=(seq, me + (1 if way == 0 else -1)), device_id_type=MESH,
        )

    def rope_copy(origin, way):
        return pltpu.make_async_remote_copy(
            src_ref=rope.at[origin], dst_ref=rope.at[origin],
            send_sem=send_rope.at[way, origin], recv_sem=recv_rope.at[origin],
            device_id=(seq, me + (1 if way == 0 else -1)), device_id_type=MESH,
        )

    def can_send(way):
        return me < n - 1 if way == 0 else me > 0

    for way in range(2):
        @pl.when(can_send(way))
        def _():
            rope_copy(me, way).start()
            latent_copy(me, 0, way).start()
            latent_copy(me, 1, way).start()

    for copy in rest:
        copy.wait()

    def scores(g, variant, key):
        query = jnp.concatenate(
            [
                qlat[pl.ds(g * group, group)].reshape(group * rows, width),
                qrest[variant, pl.ds(g * group, group)].reshape(group * rows, -1),
            ],
            axis=1,
        )
        return lax.dot_general(
            query, key, (((1,), (1,)), ((), ())), preferred_element_type=jnp.float32
        )

    def own_step(g, carry):
        key = jnp.concatenate([own_l[...], own_r[...], jnp.zeros((rows, bias.shape[2]), own_r.dtype)], axis=1)
        s = scores(g, 0, key) * scale
        s = s.reshape(group, rows, rows)
        place = lax.broadcasted_iota(jnp.int32, (group, rows, rows), 1)
        column = lax.broadcasted_iota(jnp.int32, (group, rows, rows), 2)
        s = jnp.where(column <= place, s, NEG).reshape(group * rows, rows)
        high = jnp.max(s, axis=1, keepdims=True)
        p = jnp.exp2(s - high)
        span = pl.ds(g * group * rows, group * rows)
        top[span] = jnp.broadcast_to(high, (group * rows, top.shape[1]))
        total[span] = jnp.broadcast_to(
            jnp.sum(p, axis=1, keepdims=True), (group * rows, top.shape[1])
        )
        acc[span] = jnp.dot(
            p.astype(jnp.bfloat16), own_l[...], preferred_element_type=jnp.float32
        )
        return carry

    lax.fori_loop(0, steps, own_step, 0)

    def work(origin, half):
        def one(g, carry):
            value = lat[origin, half]
            key = jnp.concatenate([value, rope[origin], bias[half]], axis=1)
            s = scores(g, half, key)
            span = pl.ds(g * group * rows, group * rows)
            before = top[span][:, :1]
            high = jnp.maximum(before, jnp.max(s, axis=1, keepdims=True) * scale)
            p = jnp.exp2(s * scale - high)
            fade = jnp.exp2(before - high)
            top[span] = jnp.broadcast_to(high, (group * rows, top.shape[1]))
            total[span] = total[span] * fade + jnp.sum(p, axis=1, keepdims=True)
            acc[span] = acc[span] * fade + jnp.dot(
                p.astype(jnp.bfloat16), value, preferred_element_type=jnp.float32
            )
            return carry

        lax.fori_loop(0, steps, one, 0)

    def own_half(half, carry):
        work(me, half)
        return carry

    lax.fori_loop(0, 2, own_half, 0)

    def slot(k, carry):
        far = 1 + k // 2
        half = k % 2
        for way in range(2):
            origin = me - far if way == 0 else me + far
            here = origin >= 0 if way == 0 else origin < n

            @pl.when(here)
            def _():
                @pl.when(half == 0)
                def _():
                    rope_copy(origin, way).wait_recv()

                latent_copy(origin, half, way).wait_recv()

                @pl.when(can_send(way))
                def _():
                    @pl.when(half == 0)
                    def _():
                        rope_copy(origin, way).start()

                    latent_copy(origin, half, way).start()

        def side(way, carry):
            origin = jnp.where(way == 0, me - far, me + far)

            @pl.when(jnp.logical_and(origin >= 0, origin < n))
            def _():
                work(origin, half)

            return carry

        lax.fori_loop(0, 2, side, 0)
        return carry

    lax.fori_loop(0, 2 * (n - 1), slot, 0)

    def finish(h, carry):
        span = pl.ds(h * rows, rows)
        mixed = (acc[span] / total[span][:, :1]).astype(jnp.bfloat16)
        out_ref[h] = jnp.dot(
            mixed, wuv[h], preferred_element_type=jnp.float32
        ).astype(jnp.bfloat16)
        return carry

    lax.fori_loop(0, heads, finish, 0)

    for far in range(n):
        for way in range(2):
            origin = me - far if way == 0 else me + far
            here = origin >= 0 if way == 0 else origin < n

            @pl.when(jnp.logical_and(here, can_send(way)))
            def _():
                rope_copy(origin, way).wait_send()
                latent_copy(origin, 0, way).wait_send()
                latent_copy(origin, 1, way).wait_send()


def attention(n, scale, lat, rope, own_lat, own_rope, bias, qlat, qrest, wuv):
    heads, rows, width = qlat.shape
    keys = lat.shape[1]
    group = 2 if heads % 2 == 0 else 1
    bf = jnp.bfloat16
    every = heads * rows
    flops = 2 * every * (keys * 2 * n + rows) * (2 * width + rope.shape[1] // 2)
    return pl.pallas_call(
        functools.partial(attention_kernel, n, group, scale),
        out_shape=jax.ShapeDtypeStruct((heads, rows, wuv.shape[2]), bf),
        in_specs=[pl.BlockSpec(memory_space=pl.ANY)] * 8,
        out_specs=pl.BlockSpec(memory_space=pltpu.VMEM),
        scratch_shapes=[
            pltpu.VMEM((n,) + lat.shape, bf),
            pltpu.VMEM((n,) + rope.shape, bf),
            pltpu.VMEM(own_lat.shape, bf),
            pltpu.VMEM(own_rope.shape, bf),
            pltpu.VMEM(bias.shape, bf),
            pltpu.VMEM(qlat.shape, bf),
            pltpu.VMEM(qrest.shape, bf),
            pltpu.VMEM(wuv.shape, bf),
            pltpu.VMEM((every, width), jnp.float32),
            pltpu.VMEM((every, 128), jnp.float32),
            pltpu.VMEM((every, 128), jnp.float32),
            pltpu.SemaphoreType.DMA((8,)),
            pltpu.SemaphoreType.DMA((n, 2)),
            pltpu.SemaphoreType.DMA((n,)),
            pltpu.SemaphoreType.DMA((2, n, 2)),
            pltpu.SemaphoreType.DMA((2, n)),
        ],
        compiler_params=pltpu.CompilerParams(
            collective_id=0, has_side_effects=True, vmem_limit_bytes=56 * 1024 * 1024
        ),
        cost_estimate=pl.CostEstimate(
            flops=flops, bytes_accessed=16 * 1024 * 1024, transcendentals=every * keys * 2 * n
        ),
    )(lat, rope, own_lat, own_rope, bias, qlat, qrest, wuv)


def per_device(queries, own_latent, cache, block_list, offsets, tile_mask, w_uk, w_uv, w_o):
    seq_count = lax.axis_size("seq")
    n = lax.axis_size("head")
    seq_index = lax.axis_index("seq")
    spans_held, part_rows, full = cache.shape
    listed = block_list.shape[1]
    heads, nope, width = w_uk.shape
    rope_width = full - width
    rows = own_latent.shape[0]
    bf = jnp.bfloat16

    owners = block_list // spans_held
    within = block_list % spans_held
    earlier = jnp.tril(jnp.ones((listed, listed), jnp.bool_), -1)
    same_owner = owners[:, :, None] == owners[:, None, :]
    ranking = jnp.sum(same_owner & earlier[None], axis=2)
    slot_ids = jnp.arange(MOST, dtype=jnp.int32)
    matches = (owners == seq_index)[:, :, None] & (ranking[:, :, None] == slot_ids[None, None, :])
    send_index = jnp.sum(jnp.where(matches, within[:, :, None], 0), axis=1)
    my_owners = lax.dynamic_index_in_dim(owners, seq_index, 0, keepdims=False)
    my_ranking = lax.dynamic_index_in_dim(ranking, seq_index, 0, keepdims=False)
    flat_slot = my_owners * MOST + my_ranking
    arrived = lax.all_to_all(cache[send_index], "seq", split_axis=0, concat_axis=0, tiled=True)
    blocks = arrived.reshape(seq_count * MOST, part_rows, full)[flat_slot]

    keys = listed * part_rows // 2
    lat = blocks[..., :width].reshape(2, keys, width)
    turned = rotate(blocks[..., width:], offsets[0]).reshape(2, keys, rope_width)
    rope = jnp.concatenate([turned[0], turned[1]], axis=1)

    tiles = tile_mask[0]
    tile_count = tiles.shape[0]
    pad = 128
    penalty = jnp.where(tiles > 0, 0.0, NEG).astype(bf)
    bias = jnp.repeat(penalty.T, part_rows, axis=0).reshape(2, keys, tile_count)
    bias = jnp.pad(bias, ((0, 0), (0, 0), (0, pad - tile_count)))

    own_lat = own_latent[:, :width]
    own_rope = jnp.pad(own_latent[:, width:], ((0, 0), (0, rope_width)))

    grouped = jnp.transpose(queries.reshape(rows, heads, nope + rope_width), (1, 0, 2))
    qlat = jnp.einsum(
        "htn,hnl->htl", grouped[..., :nope], w_uk, preferred_element_type=jnp.float32
    ).astype(bf)
    qrope = grouped[..., nope:]
    nothing = jnp.zeros_like(qrope)
    tile_of = jnp.arange(rows) // (rows // tile_count)
    which = (tile_of[:, None] == jnp.arange(pad)[None, :]).astype(bf)
    which = jnp.broadcast_to(which[None], (heads, rows, pad))
    qrest = jnp.stack(
        [
            jnp.concatenate([qrope, nothing, which], axis=2),
            jnp.concatenate([nothing, qrope, which], axis=2),
        ]
    )
    scale = (nope + rope_width) ** -0.5 * math.log2(math.e)
    per_head = attention(n, scale, lat, rope, own_lat, own_rope, bias, qlat, qrest, w_uv)
    head_out = jnp.transpose(per_head, (1, 0, 2)).reshape(rows, -1)
    partial_value = jnp.dot(head_out, w_o, preferred_element_type=jnp.float32)
    return lax.psum_scatter(
        partial_value.astype(bf), "head", scatter_dimension=1, tiled=True
    )


def solution(mesh):
    placed = (
        P("seq", "head"),
        P("seq", None),
        P("seq", "head", None),
        P(),
        P("seq", None),
        P("seq", None, None),
        P("head", None, None),
        P("head", None, None),
        P("head", None),
    )
    return jax.shard_map(
        per_device, mesh=mesh, in_specs=placed, out_specs=P("seq", "head"), check_vma=False
    )
```

```python
import functools
import math

import jax
import jax.numpy as jnp
from jax import lax
from jax.experimental import pallas as pl
from jax.experimental.pallas import tpu as pltpu
from jax.sharding import PartitionSpec as P

MOST = 4
THETA = 50000.0
MESH = pl.DeviceIdType.MESH
NEG = -1e30


def rotate(rotary, shift):
    width = rotary.shape[-1]
    halfway = width // 2
    inverse = THETA ** (-jnp.arange(halfway, dtype=jnp.float32) * 2.0 / width)
    angles = shift.astype(jnp.float32)[:, None] * inverse[None, :]
    cosine = jnp.cos(angles)[:, None, :]
    sine = jnp.sin(angles)[:, None, :]
    rotary = rotary.astype(jnp.float32)
    first = rotary[..., :halfway]
    second = rotary[..., halfway:]
    turned = jnp.concatenate(
        [first * cosine - second * sine, second * cosine + first * sine], axis=-1
    )
    return turned.astype(jnp.bfloat16)


def attention_kernel(
    n, group, scale,
    lat_in, rope_in, own_lat, own_rope, bias_in, qlat_in, qrest_in, wuv_in,
    out_ref,
    lat, rope, own_l, own_r, bias, qlat, qrest, wuv, acc, top, total,
    load_sem, recv_lat, recv_rope, send_lat, send_rope,
):
    seq = lax.axis_index("seq")
    me = lax.axis_index("head")
    heads, rows, width = qlat.shape
    keys = lat.shape[2]
    steps = heads // group
    batch = 4 if steps % 4 == 0 else 1

    mine = [
        pltpu.make_async_copy(lat_in, lat.at[me], load_sem.at[0]),
        pltpu.make_async_copy(rope_in, rope.at[me], load_sem.at[1]),
    ]
    rest = [
        pltpu.make_async_copy(src, dst, load_sem.at[2 + i])
        for i, (src, dst) in enumerate(
            [(own_lat, own_l), (own_rope, own_r), (bias_in, bias), (qlat_in, qlat),
             (qrest_in, qrest), (wuv_in, wuv)]
        )
    ]
    for copy in mine + rest:
        copy.start()

    barrier = pltpu.get_barrier_semaphore()

    @pl.when(me > 0)
    def _():
        pl.semaphore_signal(barrier, inc=1, device_id=(seq, me - 1), device_id_type=MESH)

    @pl.when(me < n - 1)
    def _():
        pl.semaphore_signal(barrier, inc=1, device_id=(seq, me + 1), device_id_type=MESH)

    peers = jnp.where(me > 0, 1, 0) + jnp.where(me < n - 1, 1, 0)
    pl.semaphore_wait(barrier, peers)

    for copy in mine:
        copy.wait()

    def latent_copy(origin, half, way):
        return pltpu.make_async_remote_copy(
            src_ref=lat.at[origin, half], dst_ref=lat.at[origin, half],
            send_sem=send_lat.at[way, origin, half], recv_sem=recv_lat.at[origin, half],
            device_id=(seq, me + (1 if way == 0 else -1)), device_id_type=MESH,
        )

    def rope_copy(origin, way):
        return pltpu.make_async_remote_copy(
            src_ref=rope.at[origin], dst_ref=rope.at[origin],
            send_sem=send_rope.at[way, origin], recv_sem=recv_rope.at[origin],
            device_id=(seq, me + (1 if way == 0 else -1)), device_id_type=MESH,
        )

    def can_send(way):
        return me < n - 1 if way == 0 else me > 0

    for way in range(2):
        @pl.when(can_send(way))
        def _():
            rope_copy(me, way).start()
            latent_copy(me, 0, way).start()
            latent_copy(me, 1, way).start()

    for copy in rest:
        copy.wait()

    def scores(g, variant, key):
        query = jnp.concatenate(
            [
                qlat[pl.ds(g * group, group)].reshape(group * rows, width),
                qrest[variant, pl.ds(g * group, group)].reshape(group * rows, -1),
            ],
            axis=1,
        )
        return lax.dot_general(
            query, key, (((1,), (1,)), ((), ())), preferred_element_type=jnp.float32
        )

    def own_step(g, carry):
        key = jnp.concatenate([own_l[...], own_r[...], jnp.zeros((rows, bias.shape[2]), own_r.dtype)], axis=1)
        s = scores(g, 0, key) * scale
        s = s.reshape(group, rows, rows)
        place = lax.broadcasted_iota(jnp.int32, (group, rows, rows), 1)
        column = lax.broadcasted_iota(jnp.int32, (group, rows, rows), 2)
        s = jnp.where(column <= place, s, NEG).reshape(group * rows, rows)
        high = jnp.max(s, axis=1, keepdims=True)
        p = jnp.exp2(s - high)
        span = pl.ds(g * group * rows, group * rows)
        top[span] = jnp.broadcast_to(high, (group * rows, top.shape[1]))
        total[span] = jnp.broadcast_to(
            jnp.sum(p, axis=1, keepdims=True), (group * rows, top.shape[1])
        )
        acc[span] = jnp.dot(
            p.astype(jnp.bfloat16), own_l[...], preferred_element_type=jnp.float32
        )
        return carry

    lax.fori_loop(0, steps, own_step, 0)

    def work(origin, half):
        value = lat[origin, half]
        key = jnp.concatenate([value, rope[origin], bias[half]], axis=1)

        def soft(g, s):
            span = pl.ds(g * group * rows, group * rows)
            before = top[span][:, :1]
            high = jnp.maximum(before, jnp.max(s, axis=1, keepdims=True) * scale)
            p = jnp.exp2(s * scale - high)
            fade = jnp.exp2(before - high)
            top[span] = jnp.broadcast_to(high, (group * rows, top.shape[1]))
            total[span] = total[span] * fade + jnp.sum(p, axis=1, keepdims=True)
            acc[span] = acc[span] * fade + jnp.dot(
                p.astype(jnp.bfloat16), value, preferred_element_type=jnp.float32
            )

        def some(i, carry):
            ahead = scores(i * batch, half, key)
            for j in range(batch):
                s = ahead
                if j + 1 < batch:
                    ahead = scores(i * batch + j + 1, half, key)
                soft(i * batch + j, s)
            return carry

        lax.fori_loop(0, steps // batch, some, 0)

    def own_half(half, carry):
        work(me, half)
        return carry

    lax.fori_loop(0, 2, own_half, 0)

    def slot(k, carry):
        far = 1 + k // 2
        half = k % 2
        for way in range(2):
            origin = me - far if way == 0 else me + far
            here = origin >= 0 if way == 0 else origin < n

            @pl.when(here)
            def _():
                @pl.when(half == 0)
                def _():
                    rope_copy(origin, way).wait_recv()

                latent_copy(origin, half, way).wait_recv()

                @pl.when(can_send(way))
                def _():
                    @pl.when(half == 0)
                    def _():
                        rope_copy(origin, way).start()

                    latent_copy(origin, half, way).start()

        def side(way, carry):
            origin = jnp.where(way == 0, me - far, me + far)

            @pl.when(jnp.logical_and(origin >= 0, origin < n))
            def _():
                work(origin, half)

            return carry

        lax.fori_loop(0, 2, side, 0)
        return carry

    lax.fori_loop(0, 2 * (n - 1), slot, 0)

    def finish(h, carry):
        span = pl.ds(h * rows, rows)
        mixed = (acc[span] / total[span][:, :1]).astype(jnp.bfloat16)
        value_width = wuv.shape[2]
        columns = pl.ds(pl.multiple_of(h * value_width, value_width), value_width)
        out_ref[:, columns] = jnp.dot(
            mixed, wuv[h], preferred_element_type=jnp.float32
        ).astype(jnp.bfloat16)
        return carry

    lax.fori_loop(0, heads, finish, 0)

    for far in range(n):
        for way in range(2):
            origin = me - far if way == 0 else me + far
            here = origin >= 0 if way == 0 else origin < n

            @pl.when(jnp.logical_and(here, can_send(way)))
            def _():
                rope_copy(origin, way).wait_send()
                latent_copy(origin, 0, way).wait_send()
                latent_copy(origin, 1, way).wait_send()


def attention(n, scale, lat, rope, own_lat, own_rope, bias, qlat, qrest, wuv):
    heads, rows, width = qlat.shape
    keys = lat.shape[1]
    group = 2 if heads % 2 == 0 else 1
    bf = jnp.bfloat16
    every = heads * rows
    flops = 2 * every * (keys * 2 * n + rows) * (2 * width + rope.shape[1] // 2)
    return pl.pallas_call(
        functools.partial(attention_kernel, n, group, scale),
        out_shape=jax.ShapeDtypeStruct((rows, heads * wuv.shape[2]), bf),
        in_specs=[pl.BlockSpec(memory_space=pl.ANY)] * 8,
        out_specs=pl.BlockSpec(memory_space=pltpu.VMEM),
        scratch_shapes=[
            pltpu.VMEM((n,) + lat.shape, bf),
            pltpu.VMEM((n,) + rope.shape, bf),
            pltpu.VMEM(own_lat.shape, bf),
            pltpu.VMEM(own_rope.shape, bf),
            pltpu.VMEM(bias.shape, bf),
            pltpu.VMEM(qlat.shape, bf),
            pltpu.VMEM(qrest.shape, bf),
            pltpu.VMEM(wuv.shape, bf),
            pltpu.VMEM((every, width), jnp.float32),
            pltpu.VMEM((every, 128), jnp.float32),
            pltpu.VMEM((every, 128), jnp.float32),
            pltpu.SemaphoreType.DMA((8,)),
            pltpu.SemaphoreType.DMA((n, 2)),
            pltpu.SemaphoreType.DMA((n,)),
            pltpu.SemaphoreType.DMA((2, n, 2)),
            pltpu.SemaphoreType.DMA((2, n)),
        ],
        compiler_params=pltpu.CompilerParams(
            collective_id=0, has_side_effects=True, vmem_limit_bytes=56 * 1024 * 1024
        ),
        cost_estimate=pl.CostEstimate(
            flops=flops, bytes_accessed=16 * 1024 * 1024, transcendentals=every * keys * 2 * n
        ),
    )(lat, rope, own_lat, own_rope, bias, qlat, qrest, wuv)


def project_kernel(
    n, head_out, w_o, out_ref, weight, part, inbox, weight_sem, send_sem, recv_sem
):
    seq = lax.axis_index("seq")
    me = lax.axis_index("head")
    rows, wide = out_ref.shape
    tile = 256 if wide % 256 == 0 else 128

    def block_of(p):
        return jnp.where(2 * me < n, n - 1 - p, p)

    def fetch(p):
        columns = pl.ds(pl.multiple_of(block_of(p) * wide, 128), wide)
        return pltpu.make_async_copy(
            w_o.at[:, columns], weight.at[p % 2], weight_sem.at[p % 2]
        )

    fetch(0).start()
    barrier = pltpu.get_barrier_semaphore()

    @pl.when(me > 0)
    def _():
        pl.semaphore_signal(barrier, inc=1, device_id=(seq, me - 1), device_id_type=MESH)

    @pl.when(me < n - 1)
    def _():
        pl.semaphore_signal(barrier, inc=1, device_id=(seq, me + 1), device_id_type=MESH)

    peers = jnp.where(me > 0, 1, 0) + jnp.where(me < n - 1, 1, 0)
    pl.semaphore_wait(barrier, peers)

    def first(block, way):
        return pltpu.make_async_remote_copy(
            src_ref=part.at[block], dst_ref=inbox.at[way, block],
            send_sem=send_sem.at[way, block], recv_sem=recv_sem.at[way, block],
            device_id=(seq, me + (1 if way == 0 else -1)), device_id_type=MESH,
        )

    def onward(block, way):
        return pltpu.make_async_remote_copy(
            src_ref=inbox.at[way, block], dst_ref=inbox.at[way, block],
            send_sem=send_sem.at[way, block], recv_sem=recv_sem.at[way, block],
            device_id=(seq, me + (1 if way == 0 else -1)), device_id_type=MESH,
        )

    def compute(p, carry):
        block = block_of(p)

        @pl.when(p + 1 < n)
        def _():
            fetch(p + 1).start()

        fetch(p).wait()

        def columns_step(t, carry):
            columns = pl.ds(pl.multiple_of(t * tile, tile), tile)
            part[block, :, columns] = jnp.dot(
                head_out[...], weight[p % 2, :, columns], preferred_element_type=jnp.float32
            ).astype(jnp.bfloat16)
            return carry

        lax.fori_loop(0, wide // tile, columns_step, 0)

        @pl.when(jnp.logical_and(me == 0, block > 0))
        def _():
            first(block, 0).start()

        @pl.when(jnp.logical_and(me == n - 1, block < n - 1))
        def _():
            first(block, 1).start()

        return carry

    lax.fori_loop(0, n, compute, 0)

    def hop(k, carry):
        for way in range(2):
            block = n - 1 + me - k if way == 0 else k - (n - 1 - me)
            if way == 0:
                here = jnp.logical_and(me > 0, jnp.logical_and(block > me, block < n))
            else:
                here = jnp.logical_and(me < n - 1, jnp.logical_and(block >= 0, block < me))

            @pl.when(here)
            def _():
                onward(block, way).wait_recv()
                inbox[way, block] = (
                    inbox[way, block].astype(jnp.float32) + part[block].astype(jnp.float32)
                ).astype(jnp.bfloat16)
                onward(block, way).start()

        return carry

    lax.fori_loop(1, n - 1, hop, 0)

    @pl.when(me == 0)
    def _():
        first(me, 1).wait_recv()
        out_ref[...] = (
            part[me].astype(jnp.float32) + inbox[1, me].astype(jnp.float32)
        ).astype(jnp.bfloat16)

    @pl.when(me == n - 1)
    def _():
        first(me, 0).wait_recv()
        out_ref[...] = (
            part[me].astype(jnp.float32) + inbox[0, me].astype(jnp.float32)
        ).astype(jnp.bfloat16)

    @pl.when(jnp.logical_and(me > 0, me < n - 1))
    def _():
        first(me, 0).wait_recv()
        first(me, 1).wait_recv()
        out_ref[...] = (
            part[me].astype(jnp.float32)
            + inbox[0, me].astype(jnp.float32)
            + inbox[1, me].astype(jnp.float32)
        ).astype(jnp.bfloat16)

    for block in range(n):
        @pl.when(block > me)
        def _():
            first(block, 0).wait_send()

        @pl.when(block < me)
        def _():
            first(block, 1).wait_send()


def project(n, head_out, w_o):
    rows, depth = head_out.shape
    wide = w_o.shape[1] // n
    bf = jnp.bfloat16
    return pl.pallas_call(
        functools.partial(project_kernel, n),
        out_shape=jax.ShapeDtypeStruct((rows, wide), bf),
        in_specs=[pl.BlockSpec(memory_space=pltpu.VMEM), pl.BlockSpec(memory_space=pl.ANY)],
        out_specs=pl.BlockSpec(memory_space=pltpu.VMEM),
        scratch_shapes=[
            pltpu.VMEM((2, depth, wide), bf),
            pltpu.VMEM((n, rows, wide), bf),
            pltpu.VMEM((2, n, rows, wide), bf),
            pltpu.SemaphoreType.DMA((2,)),
            pltpu.SemaphoreType.DMA((2, n)),
            pltpu.SemaphoreType.DMA((2, n)),
        ],
        compiler_params=pltpu.CompilerParams(
            collective_id=1, has_side_effects=True, vmem_limit_bytes=48 * 1024 * 1024
        ),
        cost_estimate=pl.CostEstimate(
            flops=2 * rows * depth * wide * n, bytes_accessed=2 * depth * wide * n,
            transcendentals=0,
        ),
    )(head_out, w_o)


def per_device(queries, own_latent, cache, block_list, offsets, tile_mask, w_uk, w_uv, w_o):
    seq_count = lax.axis_size("seq")
    n = lax.axis_size("head")
    seq_index = lax.axis_index("seq")
    spans_held, part_rows, full = cache.shape
    listed = block_list.shape[1]
    heads, nope, width = w_uk.shape
    rope_width = full - width
    rows = own_latent.shape[0]
    bf = jnp.bfloat16

    owners = block_list // spans_held
    within = block_list % spans_held
    earlier = jnp.tril(jnp.ones((listed, listed), jnp.bool_), -1)
    same_owner = owners[:, :, None] == owners[:, None, :]
    ranking = jnp.sum(same_owner & earlier[None], axis=2)
    slot_ids = jnp.arange(MOST, dtype=jnp.int32)
    matches = (owners == seq_index)[:, :, None] & (ranking[:, :, None] == slot_ids[None, None, :])
    send_index = jnp.sum(jnp.where(matches, within[:, :, None], 0), axis=1)
    my_owners = lax.dynamic_index_in_dim(owners, seq_index, 0, keepdims=False)
    my_ranking = lax.dynamic_index_in_dim(ranking, seq_index, 0, keepdims=False)
    flat_slot = my_owners * MOST + my_ranking
    arrived = lax.all_to_all(cache[send_index], "seq", split_axis=0, concat_axis=0, tiled=True)
    blocks = arrived.reshape(seq_count * MOST, part_rows, full)[flat_slot]

    keys = listed * part_rows // 2
    lat = blocks[..., :width].reshape(2, keys, width)
    turned = rotate(blocks[..., width:], offsets[0]).reshape(2, keys, rope_width)
    rope = jnp.concatenate([turned[0], turned[1]], axis=1)

    tiles = tile_mask[0]
    tile_count = tiles.shape[0]
    pad = 128
    penalty = jnp.where(tiles > 0, 0.0, NEG).astype(bf)
    bias = jnp.repeat(penalty.T, part_rows, axis=0).reshape(2, keys, tile_count)
    bias = jnp.pad(bias, ((0, 0), (0, 0), (0, pad - tile_count)))

    own_lat = own_latent[:, :width]
    own_rope = jnp.pad(own_latent[:, width:], ((0, 0), (0, rope_width)))

    grouped = jnp.transpose(queries.reshape(rows, heads, nope + rope_width), (1, 0, 2))
    qlat = jnp.einsum(
        "htn,hnl->htl", grouped[..., :nope], w_uk, preferred_element_type=jnp.float32
    ).astype(bf)
    qrope = grouped[..., nope:]
    nothing = jnp.zeros_like(qrope)
    tile_of = jnp.arange(rows) // (rows // tile_count)
    which = (tile_of[:, None] == jnp.arange(pad)[None, :]).astype(bf)
    which = jnp.broadcast_to(which[None], (heads, rows, pad))
    qrest = jnp.stack(
        [
            jnp.concatenate([qrope, nothing, which], axis=2),
            jnp.concatenate([nothing, qrope, which], axis=2),
        ]
    )
    scale = (nope + rope_width) ** -0.5 * math.log2(math.e)
    head_out = attention(n, scale, lat, rope, own_lat, own_rope, bias, qlat, qrest, w_uv)
    return project(n, head_out, w_o)


def solution(mesh):
    placed = (
        P("seq", "head"),
        P("seq", None),
        P("seq", "head", None),
        P(),
        P("seq", None),
        P("seq", None, None),
        P("head", None, None),
        P("head", None, None),
        P("head", None),
    )
    return jax.shard_map(
        per_device, mesh=mesh, in_specs=placed, out_specs=P("seq", "head"), check_vma=False
    )
```

```python
import functools
import math

import jax
import jax.numpy as jnp
from jax import lax
from jax.experimental import pallas as pl
from jax.experimental.pallas import tpu as pltpu
from jax.sharding import PartitionSpec as P

MOST = 4
THETA = 50000.0
MESH = pl.DeviceIdType.MESH
NEG = -1e30


def rotate(rotary, shift):
    width = rotary.shape[-1]
    halfway = width // 2
    inverse = THETA ** (-jnp.arange(halfway, dtype=jnp.float32) * 2.0 / width)
    angles = shift.astype(jnp.float32)[:, None] * inverse[None, :]
    cosine = jnp.cos(angles)[:, None, :]
    sine = jnp.sin(angles)[:, None, :]
    rotary = rotary.astype(jnp.float32)
    first = rotary[..., :halfway]
    second = rotary[..., halfway:]
    turned = jnp.concatenate(
        [first * cosine - second * sine, second * cosine + first * sine], axis=-1
    )
    return turned.astype(jnp.bfloat16)


def attention_kernel(
    n, group, tile_rows, scale,
    lat_in, rope_in, own_lat, own_rope, bias_in, queries_in, wuk_in, wuv_in,
    out_ref,
    lat, rope, own_l, own_r, bias, queries, wuk, qlat, qrest, wuv, acc, top, total,
    load_sem, recv_lat, recv_rope, send_lat, send_rope,
):
    seq = lax.axis_index("seq")
    me = lax.axis_index("head")
    heads, rows, width = qlat.shape
    keys = lat.shape[2]
    steps = heads // group
    batch = 4 if steps % 4 == 0 else 1

    mine = [
        pltpu.make_async_copy(lat_in, lat.at[me], load_sem.at[0]),
        pltpu.make_async_copy(rope_in, rope.at[me], load_sem.at[1]),
    ]
    rest = [
        pltpu.make_async_copy(src, dst, load_sem.at[2 + i])
        for i, (src, dst) in enumerate(
            [(own_lat, own_l), (own_rope, own_r), (bias_in, bias), (queries_in, queries),
             (wuk_in, wuk), (wuv_in, wuv)]
        )
    ]
    for copy in mine + rest:
        copy.start()

    barrier = pltpu.get_barrier_semaphore()

    @pl.when(me > 0)
    def _():
        pl.semaphore_signal(barrier, inc=1, device_id=(seq, me - 1), device_id_type=MESH)

    @pl.when(me < n - 1)
    def _():
        pl.semaphore_signal(barrier, inc=1, device_id=(seq, me + 1), device_id_type=MESH)

    peers = jnp.where(me > 0, 1, 0) + jnp.where(me < n - 1, 1, 0)
    pl.semaphore_wait(barrier, peers)

    for copy in mine:
        copy.wait()

    def latent_copy(origin, half, way):
        return pltpu.make_async_remote_copy(
            src_ref=lat.at[origin, half], dst_ref=lat.at[origin, half],
            send_sem=send_lat.at[way, origin, half], recv_sem=recv_lat.at[origin, half],
            device_id=(seq, me + (1 if way == 0 else -1)), device_id_type=MESH,
        )

    def rope_copy(origin, way):
        return pltpu.make_async_remote_copy(
            src_ref=rope.at[origin], dst_ref=rope.at[origin],
            send_sem=send_rope.at[way, origin], recv_sem=recv_rope.at[origin],
            device_id=(seq, me + (1 if way == 0 else -1)), device_id_type=MESH,
        )

    def can_send(way):
        return me < n - 1 if way == 0 else me > 0

    for way in range(2):
        @pl.when(can_send(way))
        def _():
            rope_copy(me, way).start()
            latent_copy(me, 0, way).start()
            latent_copy(me, 1, way).start()

    for copy in rest:
        copy.wait()

    nope = wuk.shape[1]
    rope_width = nope // 2
    pair_width = 3 * nope
    tiles = bias_in.shape[2]
    lane = lax.broadcasted_iota(jnp.int32, (rows, nope), 1)
    mark_row = lax.broadcasted_iota(jnp.int32, (rows, tiles), 0)
    mark_lane = lax.broadcasted_iota(jnp.int32, (rows, tiles), 1)
    mark = jnp.where(mark_row // tile_rows == mark_lane, 1.0, 0.0).astype(jnp.bfloat16)

    def prepare(i, carry):
        even, odd = 2 * i, 2 * i + 1
        x = queries[:, pl.ds(pl.multiple_of(i * pair_width, 128), pair_width)]
        tail = x[:, nope:].astype(jnp.float32)
        moved = pltpu.roll(tail, 2 * nope - rope_width, 1)
        for h, plain, low, high in (
            (even, x[:, :nope], tail[:, :nope], moved[:, nope:]),
            (odd, moved[:, :nope].astype(jnp.bfloat16), moved[:, nope:], tail[:, nope:]),
        ):
            qlat[h] = jnp.dot(
                plain, wuk[h], preferred_element_type=jnp.float32
            ).astype(jnp.bfloat16)
            first = jnp.where(lane < rope_width, low, 0.0).astype(jnp.bfloat16)
            second = jnp.where(lane >= rope_width, high, 0.0).astype(jnp.bfloat16)
            qrest[0, h] = jnp.concatenate([first, mark], axis=1)
            qrest[1, h] = jnp.concatenate([second, mark], axis=1)
        return carry

    lax.fori_loop(0, heads // 2, prepare, 0)

    def scores(g, variant, key):
        query = jnp.concatenate(
            [
                qlat[pl.ds(g * group, group)].reshape(group * rows, width),
                qrest[variant, pl.ds(g * group, group)].reshape(group * rows, -1),
            ],
            axis=1,
        )
        return lax.dot_general(
            query, key, (((1,), (1,)), ((), ())), preferred_element_type=jnp.float32
        )

    def own_step(g, carry):
        key = jnp.concatenate([own_l[...], own_r[...], jnp.zeros((rows, bias.shape[2]), own_r.dtype)], axis=1)
        s = scores(g, 0, key) * scale
        s = s.reshape(group, rows, rows)
        place = lax.broadcasted_iota(jnp.int32, (group, rows, rows), 1)
        column = lax.broadcasted_iota(jnp.int32, (group, rows, rows), 2)
        s = jnp.where(column <= place, s, NEG).reshape(group * rows, rows)
        high = jnp.max(s, axis=1, keepdims=True)
        p = jnp.exp2(s - high)
        span = pl.ds(g * group * rows, group * rows)
        top[span] = jnp.broadcast_to(high, (group * rows, top.shape[1]))
        total[span] = jnp.broadcast_to(
            jnp.sum(p, axis=1, keepdims=True), (group * rows, top.shape[1])
        )
        acc[span] = jnp.dot(
            p.astype(jnp.bfloat16), own_l[...], preferred_element_type=jnp.float32
        )
        return carry

    lax.fori_loop(0, steps, own_step, 0)

    def work(origin, half):
        value = lat[origin, half]
        key = jnp.concatenate([value, rope[origin], bias[half]], axis=1)

        def soft(g, s):
            span = pl.ds(g * group * rows, group * rows)
            before = top[span][:, :1]
            high = jnp.maximum(before, jnp.max(s, axis=1, keepdims=True) * scale)
            p = jnp.exp2(s * scale - high)
            fade = jnp.exp2(before - high)
            top[span] = jnp.broadcast_to(high, (group * rows, top.shape[1]))
            total[span] = total[span] * fade + jnp.sum(p, axis=1, keepdims=True)
            acc[span] = acc[span] * fade + jnp.dot(
                p.astype(jnp.bfloat16), value, preferred_element_type=jnp.float32
            )

        def some(i, carry):
            ahead = scores(i * batch, half, key)
            for j in range(batch):
                s = ahead
                if j + 1 < batch:
                    ahead = scores(i * batch + j + 1, half, key)
                soft(i * batch + j, s)
            return carry

        lax.fori_loop(0, steps // batch, some, 0)

    def own_half(half, carry):
        work(me, half)
        return carry

    lax.fori_loop(0, 2, own_half, 0)

    def slot(k, carry):
        far = 1 + k // 2
        half = k % 2
        for way in range(2):
            origin = me - far if way == 0 else me + far
            here = origin >= 0 if way == 0 else origin < n

            @pl.when(here)
            def _():
                @pl.when(half == 0)
                def _():
                    rope_copy(origin, way).wait_recv()

                latent_copy(origin, half, way).wait_recv()

                @pl.when(can_send(way))
                def _():
                    @pl.when(half == 0)
                    def _():
                        rope_copy(origin, way).start()

                    latent_copy(origin, half, way).start()

        def side(way, carry):
            origin = jnp.where(way == 0, me - far, me + far)

            @pl.when(jnp.logical_and(origin >= 0, origin < n))
            def _():
                work(origin, half)

            return carry

        lax.fori_loop(0, 2, side, 0)
        return carry

    lax.fori_loop(0, 2 * (n - 1), slot, 0)

    def finish(h, carry):
        span = pl.ds(h * rows, rows)
        mixed = (acc[span] / total[span][:, :1]).astype(jnp.bfloat16)
        value_width = wuv.shape[2]
        columns = pl.ds(pl.multiple_of(h * value_width, value_width), value_width)
        out_ref[:, columns] = jnp.dot(
            mixed, wuv[h], preferred_element_type=jnp.float32
        ).astype(jnp.bfloat16)
        return carry

    lax.fori_loop(0, heads, finish, 0)

    for far in range(n):
        for way in range(2):
            origin = me - far if way == 0 else me + far
            here = origin >= 0 if way == 0 else origin < n

            @pl.when(jnp.logical_and(here, can_send(way)))
            def _():
                rope_copy(origin, way).wait_send()
                latent_copy(origin, 0, way).wait_send()
                latent_copy(origin, 1, way).wait_send()


def attention(n, tile_rows, scale, lat, rope, own_lat, own_rope, bias, queries, wuk, wuv):
    heads, _, width = wuk.shape
    rows = queries.shape[0]
    keys = lat.shape[1]
    group = 2 if heads % 2 == 0 else 1
    bf = jnp.bfloat16
    every = heads * rows
    flops = 2 * every * (keys * 2 * n + rows) * (2 * width + rope.shape[1] // 2)
    return pl.pallas_call(
        functools.partial(attention_kernel, n, group, tile_rows, scale),
        out_shape=jax.ShapeDtypeStruct((rows, heads * wuv.shape[2]), bf),
        in_specs=[pl.BlockSpec(memory_space=pl.ANY)] * 8,
        out_specs=pl.BlockSpec(memory_space=pltpu.VMEM),
        scratch_shapes=[
            pltpu.VMEM((n,) + lat.shape, bf),
            pltpu.VMEM((n,) + rope.shape, bf),
            pltpu.VMEM(own_lat.shape, bf),
            pltpu.VMEM(own_rope.shape, bf),
            pltpu.VMEM(bias.shape, bf),
            pltpu.VMEM(queries.shape, bf),
            pltpu.VMEM(wuk.shape, bf),
            pltpu.VMEM((heads, rows, width), bf),
            pltpu.VMEM((2, heads, rows, rope.shape[1] + bias.shape[2]), bf),
            pltpu.VMEM(wuv.shape, bf),
            pltpu.VMEM((every, width), jnp.float32),
            pltpu.VMEM((every, 128), jnp.float32),
            pltpu.VMEM((every, 128), jnp.float32),
            pltpu.SemaphoreType.DMA((8,)),
            pltpu.SemaphoreType.DMA((n, 2)),
            pltpu.SemaphoreType.DMA((n,)),
            pltpu.SemaphoreType.DMA((2, n, 2)),
            pltpu.SemaphoreType.DMA((2, n)),
        ],
        compiler_params=pltpu.CompilerParams(
            collective_id=0, has_side_effects=True, vmem_limit_bytes=56 * 1024 * 1024
        ),
        cost_estimate=pl.CostEstimate(
            flops=flops, bytes_accessed=16 * 1024 * 1024, transcendentals=every * keys * 2 * n
        ),
    )(lat, rope, own_lat, own_rope, bias, queries, wuk, wuv)


def project_kernel(
    n, head_out, w_o, out_ref, weight, part, inbox, weight_sem, send_sem, recv_sem
):
    seq = lax.axis_index("seq")
    me = lax.axis_index("head")
    rows, wide = out_ref.shape
    tile = 256 if wide % 256 == 0 else 128

    def block_of(p):
        return jnp.where(2 * me < n, n - 1 - p, p)

    def fetch(p):
        columns = pl.ds(pl.multiple_of(block_of(p) * wide, 128), wide)
        return pltpu.make_async_copy(
            w_o.at[:, columns], weight.at[p % 2], weight_sem.at[p % 2]
        )

    fetch(0).start()
    barrier = pltpu.get_barrier_semaphore()

    @pl.when(me > 0)
    def _():
        pl.semaphore_signal(barrier, inc=1, device_id=(seq, me - 1), device_id_type=MESH)

    @pl.when(me < n - 1)
    def _():
        pl.semaphore_signal(barrier, inc=1, device_id=(seq, me + 1), device_id_type=MESH)

    peers = jnp.where(me > 0, 1, 0) + jnp.where(me < n - 1, 1, 0)
    pl.semaphore_wait(barrier, peers)

    def first(block, way):
        return pltpu.make_async_remote_copy(
            src_ref=part.at[block], dst_ref=inbox.at[way, block],
            send_sem=send_sem.at[way, block], recv_sem=recv_sem.at[way, block],
            device_id=(seq, me + (1 if way == 0 else -1)), device_id_type=MESH,
        )

    def onward(block, way):
        return pltpu.make_async_remote_copy(
            src_ref=inbox.at[way, block], dst_ref=inbox.at[way, block],
            send_sem=send_sem.at[way, block], recv_sem=recv_sem.at[way, block],
            device_id=(seq, me + (1 if way == 0 else -1)), device_id_type=MESH,
        )

    def compute(p, carry):
        block = block_of(p)

        @pl.when(p + 1 < n)
        def _():
            fetch(p + 1).start()

        fetch(p).wait()

        def columns_step(t, carry):
            columns = pl.ds(pl.multiple_of(t * tile, tile), tile)
            part[block, :, columns] = jnp.dot(
                head_out[...], weight[p % 2, :, columns], preferred_element_type=jnp.float32
            ).astype(jnp.bfloat16)
            return carry

        lax.fori_loop(0, wide // tile, columns_step, 0)

        @pl.when(jnp.logical_and(me == 0, block > 0))
        def _():
            first(block, 0).start()

        @pl.when(jnp.logical_and(me == n - 1, block < n - 1))
        def _():
            first(block, 1).start()

        return carry

    lax.fori_loop(0, n, compute, 0)

    def hop(k, carry):
        for way in range(2):
            block = n - 1 + me - k if way == 0 else k - (n - 1 - me)
            if way == 0:
                here = jnp.logical_and(me > 0, jnp.logical_and(block > me, block < n))
            else:
                here = jnp.logical_and(me < n - 1, jnp.logical_and(block >= 0, block < me))

            @pl.when(here)
            def _():
                onward(block, way).wait_recv()
                inbox[way, block] = (
                    inbox[way, block].astype(jnp.float32) + part[block].astype(jnp.float32)
                ).astype(jnp.bfloat16)
                onward(block, way).start()

        return carry

    lax.fori_loop(1, n - 1, hop, 0)

    @pl.when(me == 0)
    def _():
        first(me, 1).wait_recv()
        out_ref[...] = (
            part[me].astype(jnp.float32) + inbox[1, me].astype(jnp.float32)
        ).astype(jnp.bfloat16)

    @pl.when(me == n - 1)
    def _():
        first(me, 0).wait_recv()
        out_ref[...] = (
            part[me].astype(jnp.float32) + inbox[0, me].astype(jnp.float32)
        ).astype(jnp.bfloat16)

    @pl.when(jnp.logical_and(me > 0, me < n - 1))
    def _():
        first(me, 0).wait_recv()
        first(me, 1).wait_recv()
        out_ref[...] = (
            part[me].astype(jnp.float32)
            + inbox[0, me].astype(jnp.float32)
            + inbox[1, me].astype(jnp.float32)
        ).astype(jnp.bfloat16)

    for block in range(n):
        @pl.when(block > me)
        def _():
            first(block, 0).wait_send()

        @pl.when(block < me)
        def _():
            first(block, 1).wait_send()


def project(n, head_out, w_o):
    rows, depth = head_out.shape
    wide = w_o.shape[1] // n
    bf = jnp.bfloat16
    return pl.pallas_call(
        functools.partial(project_kernel, n),
        out_shape=jax.ShapeDtypeStruct((rows, wide), bf),
        in_specs=[pl.BlockSpec(memory_space=pltpu.VMEM), pl.BlockSpec(memory_space=pl.ANY)],
        out_specs=pl.BlockSpec(memory_space=pltpu.VMEM),
        scratch_shapes=[
            pltpu.VMEM((2, depth, wide), bf),
            pltpu.VMEM((n, rows, wide), bf),
            pltpu.VMEM((2, n, rows, wide), bf),
            pltpu.SemaphoreType.DMA((2,)),
            pltpu.SemaphoreType.DMA((2, n)),
            pltpu.SemaphoreType.DMA((2, n)),
        ],
        compiler_params=pltpu.CompilerParams(
            collective_id=1, has_side_effects=True, vmem_limit_bytes=48 * 1024 * 1024
        ),
        cost_estimate=pl.CostEstimate(
            flops=2 * rows * depth * wide * n, bytes_accessed=2 * depth * wide * n,
            transcendentals=0,
        ),
    )(head_out, w_o)


def per_device(queries, own_latent, cache, block_list, offsets, tile_mask, w_uk, w_uv, w_o):
    seq_count = lax.axis_size("seq")
    n = lax.axis_size("head")
    seq_index = lax.axis_index("seq")
    spans_held, part_rows, full = cache.shape
    listed = block_list.shape[1]
    heads, nope, width = w_uk.shape
    rope_width = full - width
    rows = own_latent.shape[0]
    bf = jnp.bfloat16

    owners = block_list // spans_held
    within = block_list % spans_held
    earlier = jnp.tril(jnp.ones((listed, listed), jnp.bool_), -1)
    same_owner = owners[:, :, None] == owners[:, None, :]
    ranking = jnp.sum(same_owner & earlier[None], axis=2)
    slot_ids = jnp.arange(MOST, dtype=jnp.int32)
    matches = (owners == seq_index)[:, :, None] & (ranking[:, :, None] == slot_ids[None, None, :])
    send_index = jnp.sum(jnp.where(matches, within[:, :, None], 0), axis=1)
    my_owners = lax.dynamic_index_in_dim(owners, seq_index, 0, keepdims=False)
    my_ranking = lax.dynamic_index_in_dim(ranking, seq_index, 0, keepdims=False)
    flat_slot = my_owners * MOST + my_ranking
    arrived = lax.all_to_all(cache[send_index], "seq", split_axis=0, concat_axis=0, tiled=True)
    blocks = arrived.reshape(seq_count * MOST, part_rows, full)[flat_slot]

    keys = listed * part_rows // 2
    lat = blocks[..., :width].reshape(2, keys, width)
    turned = rotate(blocks[..., width:], offsets[0]).reshape(2, keys, rope_width)
    rope = jnp.concatenate([turned[0], turned[1]], axis=1)

    tiles = tile_mask[0]
    tile_count = tiles.shape[0]
    pad = 128
    penalty = jnp.where(tiles > 0, 0.0, NEG).astype(bf)
    bias = jnp.repeat(penalty.T, part_rows, axis=0).reshape(2, keys, tile_count)
    bias = jnp.pad(bias, ((0, 0), (0, 0), (0, pad - tile_count)))

    own_lat = own_latent[:, :width]
    own_rope = jnp.pad(own_latent[:, width:], ((0, 0), (0, rope_width)))

    scale = (nope + rope_width) ** -0.5 * math.log2(math.e)
    head_out = attention(
        n, rows // tile_count, scale, lat, rope, own_lat, own_rope, bias, queries, w_uk, w_uv
    )
    return project(n, head_out, w_o)


def solution(mesh):
    placed = (
        P("seq", "head"),
        P("seq", None),
        P("seq", "head", None),
        P(),
        P("seq", None),
        P("seq", None, None),
        P("head", None, None),
        P("head", None, None),
        P("head", None),
    )
    return jax.shard_map(
        per_device, mesh=mesh, in_specs=placed, out_specs=P("seq", "head"), check_vma=False
    )
```
